32 devices in a mesh: seq: 4 (over y, x), mp: 8 (over z, core).
Axes of the slice: x: 2, y: 2, z: 4, core: 2. Of those that a mesh axis runs over, the one named last changes fastest.
Arguments:
- queries: bfloat16 [4, 8, 1280, 256], P('seq', 'mp'), may hold values from -6 to 6
- key_rows: bfloat16 [4, 8, 1280, 128], P('seq', 'mp'), may hold values from -6 to 6
- value_rows: bfloat16 [4, 8, 1280, 128], P('seq', 'mp'), may hold values from -6 to 6
Outputs:
- attended: bfloat16 [4, 8, 1280, 256], P('seq', 'mp')
The draws below stay inside these ranges and needn't reach their ends.
All inputs are finite; a program needn't handle non-finite values.
Results may differ from the reference program's by a relative error of at most 0.0055.
Values may be sent and summed in bfloat16 or wider, within the bound.
A program may use at most 64 MiB of HBM per device.

```python
import jax
import jax.numpy as jnp
from jax import lax

HD = 128
KVH = 8
QPK = 2
WINDOW = 1024
BLOCK_ROWS = 1280
SPAN_SHARDS = 4
HEAD_ROW_PAIRS = 8
N_MP = 8


def joint_draw(key):
    folded_random = jax.random.fold_in(key, 4242)
    query_random_seed, key_random_seed = jax.random.split(folded_random, 2)
    query_shape = (SPAN_SHARDS, HEAD_ROW_PAIRS, BLOCK_ROWS, QPK, HD)
    key_shape = (SPAN_SHARDS, HEAD_ROW_PAIRS, BLOCK_ROWS, HD)
    query_draw = jax.random.truncated_normal(query_random_seed, -6.0, 6.0, query_shape, jnp.float32)
    key_draw = jax.random.truncated_normal(key_random_seed, -6.0, 6.0, key_shape, jnp.float32)
    return (query_draw.reshape(SPAN_SHARDS, HEAD_ROW_PAIRS, BLOCK_ROWS, QPK * HD), key_draw)


def draw_queries(key, part):
    return joint_draw(key)[0].astype(jnp.bfloat16)


def draw_key_rows(key, part):
    return joint_draw(key)[1].astype(jnp.bfloat16)


def level_of(key, extent, shards, low, largest):
    level = 1.0
    for dim, parts in shards:
        draws = jax.random.uniform(jax.random.fold_in(jax.random.fold_in(key, 6), dim), (parts,), jnp.float32, low / len(shards), largest / len(shards))
        level = level * jnp.repeat(jnp.exp(draws), extent[dim] // parts).reshape((-1,) + (1,) * (len(extent) - 1 - dim))
    return level


def gaussian(stream_key, dims, spread, bound, shards=(), kind=jnp.bfloat16):
    values = jax.random.normal(stream_key, dims, jnp.float32) * spread
    if len(shards) > 0:
        values = level_of(stream_key, dims, shards, -0.22, 0.18) * values
    return jnp.clip(values, min=-bound, max=bound).astype(kind)


def setup_inputs(seed: int = 0) -> dict:
    key_of = jax.random.split(jax.random.key(seed), 4)
    queries = draw_queries(jax.random.fold_in(key_of[3], 71), 0)
    key_rows = draw_key_rows(jax.random.fold_in(key_of[3], 71), 0)
    value_rows = gaussian(key_of[2], (SPAN_SHARDS, HEAD_ROW_PAIRS, BLOCK_ROWS, HD), 1.0, 6.0, ((0, 4), (1, 8)))
    return dict(queries=queries, key_rows=key_rows, value_rows=value_rows)


scale_factor = 168.0 ** -0.5


def regroup(grouped_in, last_width):
    block_count = N_MP // KVH
    return grouped_in.reshape(SPAN_SHARDS * block_count, KVH, BLOCK_ROWS, last_width)


def reference(queries, key_rows, value_rows):
    block_count = N_MP // KVH
    group_count = SPAN_SHARDS * block_count
    query_all = regroup(queries, QPK * HD).reshape(group_count, KVH, BLOCK_ROWS, QPK, HD)
    key_all = regroup(key_rows, HD)
    value_all = regroup(value_rows, HD)
    key_prior = jnp.concatenate([jnp.zeros_like(key_all[:1]), key_all[:-1]], axis=0)[:, :, BLOCK_ROWS - WINDOW:]
    value_prior = jnp.concatenate([jnp.zeros_like(value_all[:1]), value_all[:-1]], axis=0)[:, :, BLOCK_ROWS - WINDOW:]
    numbers = jnp.arange(group_count, dtype=jnp.int32)
    query_pos = lax.broadcasted_iota(jnp.int32, (BLOCK_ROWS, WINDOW + BLOCK_ROWS), 0)
    key_pos = lax.broadcasted_iota(jnp.int32, (BLOCK_ROWS, WINDOW + BLOCK_ROWS), 1) - WINDOW
    base_valid = (key_pos <= query_pos) & (query_pos - key_pos < WINDOW)

    def one_block(packed):
        query_group, key_group, key_before, value_group, value_before, block_number = packed
        keys_all = jnp.concatenate([key_before, key_group], axis=1).astype(jnp.float32)
        values_all = jnp.concatenate([value_before, value_group], axis=1).astype(jnp.float32)
        scores = jnp.einsum("hrpd,hkd->hprk", query_group.astype(jnp.float32), keys_all) * scale_factor
        valid = base_valid & ((key_pos >= 0) | (block_number > 0))
        scores = jnp.where(valid, scores, -jnp.inf)
        row_top = jnp.max(scores, axis=-1, keepdims=True)
        probable = jnp.exp(scores - row_top)
        row_total = jnp.sum(probable, axis=-1, keepdims=True)
        weights = lax.optimization_barrier(probable.astype(jnp.bfloat16)).astype(jnp.float32)
        context = jnp.einsum("hprk,hkd->hprd", weights, values_all) / row_total
        context = jnp.transpose(context, (0, 2, 1, 3)).astype(jnp.bfloat16)
        return context.reshape(KVH, BLOCK_ROWS, QPK * HD)

    result = lax.map(one_block, (query_all, key_all, key_prior, value_all, value_prior, numbers))
    return result.reshape(SPAN_SHARDS, block_count * KVH, BLOCK_ROWS, QPK * HD)
```

```python
import functools
import math

import jax
import jax.numpy as jnp
from jax import lax
from jax.experimental import pallas as pl
from jax.experimental.pallas import tpu as pltpu
from jax.sharding import PartitionSpec as P

KVH = 8
QPK = 2
WINDOW = 1024
TILE = 256
LOG2_SCALE = 168.0 ** (-0.5) * math.log2(math.e)
LOWEST = -1e30


def attention_kernel(
    seq_count, mp_count, q_hbm, k_hbm, v_hbm, o_hbm, q_rows, keys, values, o_rows, in_sem, out_sem, send_sem, recv_sem
):
    rows = q_hbm.shape[2]
    head = k_hbm.shape[3]
    blocks_here = mp_count // KVH
    total = seq_count * blocks_here
    chunks = WINDOW // TILE
    q_blocks = rows // TILE
    mp_index = lax.axis_index("mp")
    kv_head = mp_index % KVH
    group = lax.axis_index("seq") * blocks_here + mp_index // KVH
    opening = group == 0
    closing = group == total - 1

    def device_of(number):
        return (number // blocks_here, (number % blocks_here) * KVH + kv_head)

    following = device_of((group + 1) % total)
    previous = device_of((group + total - 1) % total)

    barrier = pltpu.get_barrier_semaphore()

    @pl.when(jnp.logical_not(opening))
    def _():
        pl.semaphore_signal(barrier, inc=1, device_id=previous, device_id_type=pl.DeviceIdType.MESH)

    loads = [
        pltpu.make_async_copy(k_hbm.at[0, 0], keys.at[pl.ds(WINDOW, rows)], in_sem.at[0]),
        pltpu.make_async_copy(q_hbm.at[0, 0], q_rows, in_sem.at[1]),
        pltpu.make_async_copy(v_hbm.at[0, 0], values.at[pl.ds(WINDOW, rows)], in_sem.at[2]),
    ]
    for load in loads:
        load.start()

    def halo_copies(chunk):
        made = []
        for which, (source, target) in enumerate(((k_hbm, keys), (v_hbm, values))):
            made.append(
                pltpu.make_async_remote_copy(
                    src_ref=source.at[0, 0, pl.ds(rows - WINDOW + chunk * TILE, TILE)],
                    dst_ref=target.at[pl.ds(chunk * TILE, TILE)],
                    send_sem=send_sem.at[chunk, which],
                    recv_sem=recv_sem.at[chunk, which],
                    device_id=following,
                    device_id_type=pl.DeviceIdType.MESH,
                )
            )
        return made

    copies = [halo_copies(chunk) for chunk in range(chunks)]

    @pl.when(jnp.logical_not(closing))
    def _():
        pl.semaphore_wait(barrier, 1)
        for chunk in reversed(range(chunks)):
            for copy in copies[chunk]:
                copy.start()

    @pl.when(opening)
    def _():
        keys[0:WINDOW, :] = jnp.zeros((WINDOW, head), jnp.bfloat16)
        values[0:WINDOW, :] = jnp.zeros((WINDOW, head), jnp.bfloat16)

    halo_bias = jnp.where(opening, LOWEST, 0.0).astype(jnp.float32)

    def arrive(chunk):
        @pl.when(jnp.logical_not(opening))
        def _():
            for copy in copies[chunk]:
                copy.wait_recv()

    row_index = lax.broadcasted_iota(jnp.int32, (TILE, TILE), 0)
    column_index = lax.broadcasted_iota(jnp.int32, (TILE, TILE), 1)

    def part(block, sub_head, first, last):
        query = q_rows[block * TILE : (block + 1) * TILE, sub_head * head : (sub_head + 1) * head]
        tiles = []
        for step in range(first, last):
            place = (block + step) * TILE
            raw = lax.dot_general(
                query, keys[place : place + TILE, :], (((1,), (1,)), ((), ())), preferred_element_type=jnp.float32
            )
            if step == 0:
                raw = jnp.where(column_index > row_index, raw, LOWEST)
            if step == chunks:
                raw = jnp.where(column_index <= row_index, raw, LOWEST)
            tiles.append(raw)
        halo_tiles = min(max(chunks - block - first, 0), last - first)
        top = None
        if halo_tiles > 0:
            top = functools.reduce(jnp.maximum, tiles[:halo_tiles])
            top = jnp.max(top, axis=1, keepdims=True) + halo_bias
        if halo_tiles < len(tiles):
            local_top = functools.reduce(jnp.maximum, tiles[halo_tiles:])
            local_top = jnp.max(local_top, axis=1, keepdims=True)
            top = local_top if top is None else jnp.maximum(top, local_top)
        return tiles, halo_tiles, top

    def weigh(block, first, tiles, halo_tiles, top):
        shift = top * LOG2_SCALE
        halo_shift = shift - halo_bias
        lane_total = None
        gathered = None
        for number, raw in enumerate(tiles):
            probable = jnp.exp2(raw * LOG2_SCALE - (halo_shift if number < halo_tiles else shift))
            lane_total = probable if lane_total is None else lane_total + probable
            place = (block + first + number) * TILE
            term = jnp.dot(
                probable.astype(jnp.bfloat16), values[place : place + TILE, :], preferred_element_type=jnp.float32
            )
            gathered = term if gathered is None else gathered + term
        return jnp.sum(lane_total, axis=1, keepdims=True), gathered

    def store_out(block):
        return pltpu.make_async_copy(
            o_rows.at[pl.ds(block * TILE, TILE)], o_hbm.at[0, 0, pl.ds(block * TILE, TILE)], out_sem.at[block]
        )

    def finish(block, sub_head, row_total, gathered):
        o_rows[block * TILE : (block + 1) * TILE, sub_head * head : (sub_head + 1) * head] = (
            gathered / row_total
        ).astype(jnp.bfloat16)

    for load in loads:
        load.wait()

    held = []
    for block in reversed(range(q_blocks)):
        if 0 < block < chunks:
            arrive(block)
        for sub_head in range(QPK):
            first = 1 if block == 0 else 0
            tiles, halo_tiles, top = part(block, sub_head, first, chunks + 1)
            row_total, gathered = weigh(block, first, tiles, halo_tiles, top)
            if block == 0:
                held.append((top, row_total, gathered))
            else:
                finish(block, sub_head, row_total, gathered)
        if block > 0:
            store_out(block).start()
    arrive(0)
    for sub_head in range(QPK):
        top, row_total, gathered = held[sub_head]
        tiles, halo_tiles, edge_top = part(0, sub_head, 0, 1)
        new_top = jnp.maximum(top, edge_top)
        keep = jnp.exp2((top - new_top) * LOG2_SCALE)
        edge_total, edge_gathered = weigh(0, 0, tiles, halo_tiles, new_top)
        finish(0, sub_head, row_total * keep + edge_total, gathered * keep + edge_gathered)
    store_out(0).start()

    @pl.when(jnp.logical_not(closing))
    def _():
        for chunk in reversed(range(chunks)):
            for copy in copies[chunk]:
                copy.wait_send()

    for block in reversed(range(q_blocks)):
        store_out(block).wait()


def solution(mesh):
    seq_count = mesh.shape["seq"]
    mp_count = mesh.shape["mp"]

    def per_device(queries, key_rows, value_rows):
        rows = queries.shape[2]
        head = key_rows.shape[3]
        span = rows + WINDOW
        return pl.pallas_call(
            functools.partial(attention_kernel, seq_count, mp_count),
            out_shape=jax.ShapeDtypeStruct(queries.shape, jnp.bfloat16),
            in_specs=[pl.BlockSpec(memory_space=pltpu.HBM)] * 3,
            out_specs=pl.BlockSpec(memory_space=pl.ANY),
            scratch_shapes=[
                pltpu.VMEM((rows, QPK * head), jnp.bfloat16),
                pltpu.VMEM((span, head), jnp.bfloat16),
                pltpu.VMEM((span, head), jnp.bfloat16),
                pltpu.VMEM((rows, QPK * head), jnp.bfloat16),
                pltpu.SemaphoreType.DMA((3,)),
                pltpu.SemaphoreType.DMA((rows // TILE,)),
                pltpu.SemaphoreType.DMA((WINDOW // TILE, 2)),
                pltpu.SemaphoreType.DMA((WINDOW // TILE, 2)),
            ],
            compiler_params=pltpu.CompilerParams(
                collective_id=0, has_side_effects=True, vmem_limit_bytes=32 * 1024 * 1024
            ),
            cost_estimate=pl.CostEstimate(
                flops=4 * QPK * rows * (WINDOW + TILE) * head,
                bytes_accessed=6 * rows * QPK * head,
                transcendentals=QPK * rows * (WINDOW + TILE),
            ),
        )(queries, key_rows, value_rows)

    spec = P("seq", "mp", None, None)
    return jax.shard_map(per_device, mesh=mesh, in_specs=(spec, spec, spec), out_specs=spec, check_vma=False)
```

```python
import functools
import math

import jax
import jax.numpy as jnp
from jax import lax
from jax.experimental import pallas as pl
from jax.experimental.pallas import tpu as pltpu
from jax.sharding import PartitionSpec as P

KVH = 8
QPK = 2
WINDOW = 1024
TILE = 256
PIECE = 128
IN_FLIGHT = 3
LOG2_SCALE = 168.0 ** (-0.5) * math.log2(math.e)
LOWEST = -1e30


def attention_kernel(
    seq_count, mp_count, q_hbm, k_hbm, v_hbm, o_rows, q_rows, keys, values, in_sem, send_sem, recv_sem
):
    rows = q_hbm.shape[2]
    head = k_hbm.shape[3]
    blocks_here = mp_count // KVH
    total = seq_count * blocks_here
    chunks = WINDOW // TILE
    q_blocks = rows // TILE
    mp_index = lax.axis_index("mp")
    kv_head = mp_index % KVH
    group = lax.axis_index("seq") * blocks_here + mp_index // KVH
    opening = group == 0
    closing = group == total - 1

    def device_of(number):
        return (number // blocks_here, (number % blocks_here) * KVH + kv_head)

    following = device_of((group + 1) % total)
    previous = device_of((group + total - 1) % total)

    barrier = pltpu.get_barrier_semaphore()

    @pl.when(jnp.logical_not(opening))
    def _():
        pl.semaphore_signal(barrier, inc=1, device_id=previous, device_id_type=pl.DeviceIdType.MESH)

    loads = [
        pltpu.make_async_copy(k_hbm.at[0, 0], keys.at[pl.ds(WINDOW, rows)], in_sem.at[0]),
        pltpu.make_async_copy(q_hbm.at[0, 0], q_rows, in_sem.at[1]),
        pltpu.make_async_copy(v_hbm.at[0, 0], values.at[pl.ds(WINDOW, rows)], in_sem.at[2]),
    ]
    for load in loads:
        load.start()

    def halo_copies(piece):
        first = WINDOW - (piece + 1) * PIECE
        made = []
        for which, (source, target) in enumerate(((k_hbm, keys), (v_hbm, values))):
            made.append(
                pltpu.make_async_remote_copy(
                    src_ref=source.at[0, 0, pl.ds(rows - WINDOW + first, PIECE)],
                    dst_ref=target.at[pl.ds(first, PIECE)],
                    send_sem=send_sem.at[piece, which],
                    recv_sem=recv_sem.at[piece, which],
                    device_id=following,
                    device_id_type=pl.DeviceIdType.MESH,
                )
            )
        return made

    pieces = WINDOW // PIECE
    copies = [halo_copies(piece) for piece in range(pieces)]

    @pl.when(jnp.logical_not(closing))
    def _():
        pl.semaphore_wait(barrier, 1)
        for piece in range(min(IN_FLIGHT, pieces)):
            for copy in copies[piece]:
                copy.start()

    def sent(piece):
        @pl.when(jnp.logical_not(closing))
        def _():
            for copy in copies[piece]:
                copy.wait_send()
            if piece + IN_FLIGHT < pieces:
                for copy in copies[piece + IN_FLIGHT]:
                    copy.start()

    @pl.when(opening)
    def _():
        keys[0:WINDOW, :] = jnp.zeros((WINDOW, head), jnp.bfloat16)
        values[0:WINDOW, :] = jnp.zeros((WINDOW, head), jnp.bfloat16)

    halo_bias = jnp.where(opening, LOWEST, 0.0).astype(jnp.float32)

    def arrive(chunk):
        per_chunk = TILE // PIECE
        for piece in range((chunks - 1 - chunk) * per_chunk, (chunks - chunk) * per_chunk):
            sent(piece)

            @pl.when(jnp.logical_not(opening))
            def _():
                for copy in copies[piece]:
                    copy.wait_recv()

    row_index = lax.broadcasted_iota(jnp.int32, (TILE, TILE), 0)
    column_index = lax.broadcasted_iota(jnp.int32, (TILE, TILE), 1)

    def part(block, sub_head, first, last):
        query = q_rows[block * TILE : (block + 1) * TILE, sub_head * head : (sub_head + 1) * head]
        tiles = []
        for step in range(first, last):
            place = (block + step) * TILE
            raw = lax.dot_general(
                query, keys[place : place + TILE, :], (((1,), (1,)), ((), ())), preferred_element_type=jnp.float32
            )
            if step == 0:
                raw = jnp.where(column_index > row_index, raw, LOWEST)
            if step == chunks:
                raw = jnp.where(column_index <= row_index, raw, LOWEST)
            tiles.append(raw)
        halo_tiles = min(max(chunks - block - first, 0), last - first)
        top = None
        if halo_tiles > 0:
            top = functools.reduce(jnp.maximum, tiles[:halo_tiles])
            top = jnp.max(top, axis=1, keepdims=True) + halo_bias
        if halo_tiles < len(tiles):
            local_top = functools.reduce(jnp.maximum, tiles[halo_tiles:])
            local_top = jnp.max(local_top, axis=1, keepdims=True)
            top = local_top if top is None else jnp.maximum(top, local_top)
        return tiles, halo_tiles, top

    def weigh(block, first, tiles, halo_tiles, top):
        shift = top * LOG2_SCALE
        halo_shift = shift - halo_bias
        lane_total = None
        gathered = None
        for number, raw in enumerate(tiles):
            probable = jnp.exp2(raw * LOG2_SCALE - (halo_shift if number < halo_tiles else shift))
            lane_total = probable if lane_total is None else lane_total + probable
            place = (block + first + number) * TILE
            term = jnp.dot(
                probable.astype(jnp.bfloat16), values[place : place + TILE, :], preferred_element_type=jnp.float32
            )
            gathered = term if gathered is None else gathered + term
        return jnp.sum(lane_total, axis=1, keepdims=True), gathered

    def finish(block, sub_head, row_total, gathered):
        o_rows[0, 0, block * TILE : (block + 1) * TILE, sub_head * head : (sub_head + 1) * head] = (
            gathered / row_total
        ).astype(jnp.bfloat16)

    for load in loads:
        load.wait()

    held = []
    for block in reversed(range(q_blocks)):
        if 0 < block < chunks:
            arrive(block)
        for sub_head in range(QPK):
            first = 1 if block == 0 else 0
            tiles, halo_tiles, top = part(block, sub_head, first, chunks + 1)
            row_total, gathered = weigh(block, first, tiles, halo_tiles, top)
            if block == 0:
                held.append((top, row_total, gathered))
            else:
                finish(block, sub_head, row_total, gathered)
    arrive(0)
    for sub_head in range(QPK):
        top, row_total, gathered = held[sub_head]
        tiles, halo_tiles, edge_top = part(0, sub_head, 0, 1)
        new_top = jnp.maximum(top, edge_top)
        keep = jnp.exp2((top - new_top) * LOG2_SCALE)
        edge_total, edge_gathered = weigh(0, 0, tiles, halo_tiles, new_top)
        finish(0, sub_head, row_total * keep + edge_total, gathered * keep + edge_gathered)


def solution(mesh):
    seq_count = mesh.shape["seq"]
    mp_count = mesh.shape["mp"]

    def per_device(queries, key_rows, value_rows):
        rows = queries.shape[2]
        head = key_rows.shape[3]
        span = rows + WINDOW
        return pl.pallas_call(
            functools.partial(attention_kernel, seq_count, mp_count),
            out_shape=jax.ShapeDtypeStruct(queries.shape, jnp.bfloat16),
            in_specs=[pl.BlockSpec(memory_space=pltpu.HBM)] * 3,
            out_specs=pl.BlockSpec(memory_space=pltpu.VMEM),
            scratch_shapes=[
                pltpu.VMEM((rows, QPK * head), jnp.bfloat16),
                pltpu.VMEM((span, head), jnp.bfloat16),
                pltpu.VMEM((span, head), jnp.bfloat16),
                pltpu.SemaphoreType.DMA((3,)),
                pltpu.SemaphoreType.DMA((WINDOW // PIECE, 2)),
                pltpu.SemaphoreType.DMA((WINDOW // PIECE, 2)),
            ],
            compiler_params=pltpu.CompilerParams(
                collective_id=0, has_side_effects=True, vmem_limit_bytes=32 * 1024 * 1024
            ),
            cost_estimate=pl.CostEstimate(
                flops=4 * QPK * rows * (WINDOW + TILE) * head,
                bytes_accessed=6 * rows * QPK * head,
                transcendentals=QPK * rows * (WINDOW + TILE),
            ),
        )(*[pltpu.with_memory_space_constraint(x, pltpu.HBM) for x in (queries, key_rows, value_rows)])

    spec = P("seq", "mp", None, None)
    return jax.shard_map(per_device, mesh=mesh, in_specs=(spec, spec, spec), out_specs=spec, check_vma=False)
```

```python
import functools
import math

import jax
import jax.numpy as jnp
from jax import lax
from jax.experimental import pallas as pl
from jax.experimental.pallas import tpu as pltpu
from jax.sharding import PartitionSpec as P

KVH = 8
QPK = 2
WINDOW = 1024
TILE = 256
PIECE = 128
IN_FLIGHT = 4
LOG2_SCALE = 168.0 ** (-0.5) * math.log2(math.e)
LOWEST = -1e30


def attention_kernel(
    seq_count, mp_count, q_hbm, k_hbm, v_hbm, o_rows, q_rows, keys, values, in_sem, send_sem, recv_sem
):
    rows = q_hbm.shape[2]
    head = k_hbm.shape[3]
    blocks_here = mp_count // KVH
    total = seq_count * blocks_here
    chunks = WINDOW // TILE
    q_blocks = rows // TILE
    mp_index = lax.axis_index("mp")
    kv_head = mp_index % KVH
    group = lax.axis_index("seq") * blocks_here + mp_index // KVH
    opening = group == 0
    closing = group == total - 1

    def device_of(number):
        return (number // blocks_here, (number % blocks_here) * KVH + kv_head)

    following = device_of((group + 1) % total)
    previous = device_of((group + total - 1) % total)

    barrier = pltpu.get_barrier_semaphore()

    @pl.when(jnp.logical_not(opening))
    def _():
        pl.semaphore_signal(barrier, inc=1, device_id=previous, device_id_type=pl.DeviceIdType.MESH)

    loads = [
        pltpu.make_async_copy(k_hbm.at[0, 0], keys.at[pl.ds(WINDOW, rows)], in_sem.at[0]),
        pltpu.make_async_copy(q_hbm.at[0, 0], q_rows, in_sem.at[1]),
        pltpu.make_async_copy(v_hbm.at[0, 0], values.at[pl.ds(WINDOW, rows)], in_sem.at[2]),
    ]
    for load in loads:
        load.start()

    def halo_copies(piece):
        first = WINDOW - (piece + 1) * PIECE
        made = []
        for which, (source, target) in enumerate(((k_hbm, keys), (v_hbm, values))):
            made.append(
                pltpu.make_async_remote_copy(
                    src_ref=source.at[0, 0, pl.ds(rows - WINDOW + first, PIECE)],
                    dst_ref=target.at[pl.ds(first, PIECE)],
                    send_sem=send_sem.at[piece, which],
                    recv_sem=recv_sem.at[piece, which],
                    device_id=following,
                    device_id_type=pl.DeviceIdType.MESH,
                )
            )
        return made

    pieces = WINDOW // PIECE
    copies = [halo_copies(piece) for piece in range(pieces)]

    @pl.when(jnp.logical_not(closing))
    def _():
        pl.semaphore_wait(barrier, 1)
        for piece in range(min(IN_FLIGHT, pieces)):
            for copy in copies[piece]:
                copy.start()

    def sent(piece):
        @pl.when(jnp.logical_not(closing))
        def _():
            for copy in copies[piece]:
                copy.wait_send()
            if piece + IN_FLIGHT < pieces:
                for copy in copies[piece + IN_FLIGHT]:
                    copy.start()

    @pl.when(opening)
    def _():
        keys[0:WINDOW, :] = jnp.zeros((WINDOW, head), jnp.bfloat16)
        values[0:WINDOW, :] = jnp.zeros((WINDOW, head), jnp.bfloat16)

    halo_bias = jnp.where(opening, LOWEST, 0.0).astype(jnp.float32)

    def arrive(chunk):
        per_chunk = TILE // PIECE
        for piece in range((chunks - 1 - chunk) * per_chunk, (chunks - chunk) * per_chunk):
            sent(piece)

            @pl.when(jnp.logical_not(opening))
            def _():
                for copy in copies[piece]:
                    copy.wait_recv()

    stacked = QPK * TILE
    row_index = lax.broadcasted_iota(jnp.int32, (stacked, TILE), 0) % TILE
    column_index = lax.broadcasted_iota(jnp.int32, (stacked, TILE), 1)

    def scores_of(query, block, step):
        place = (block + step) * TILE
        raw = lax.dot_general(
            query, keys[place : place + TILE, :], (((1,), (1,)), ((), ())), preferred_element_type=jnp.float32
        )
        if step == 0:
            raw = jnp.where(column_index > row_index, raw, LOWEST)
        if step == chunks:
            raw = jnp.where(column_index <= row_index, raw, LOWEST)
        return raw

    def weighed(tiles, shift):
        lane_total = None
        gathered = None
        for place, raw in tiles:
            probable = jnp.exp2(raw * LOG2_SCALE - shift)
            lane_total = probable if lane_total is None else lane_total + probable
            term = jnp.dot(
                probable.astype(jnp.bfloat16), values[place : place + TILE, :], preferred_element_type=jnp.float32
            )
            gathered = term if gathered is None else gathered + term
        return jnp.sum(lane_total, axis=1, keepdims=True), gathered

    def stacked_query(block):
        both = q_rows[block * TILE : (block + 1) * TILE, :]
        return jnp.concatenate([both[:, part * head : (part + 1) * head] for part in range(QPK)], axis=0)

    def local_part(block):
        query = stacked_query(block)
        tiles = [
            ((block + step) * TILE, scores_of(query, block, step))
            for step in range(max(chunks - block, 0), chunks + 1)
        ]
        top = jnp.max(functools.reduce(jnp.maximum, [raw for _, raw in tiles]), axis=1, keepdims=True)
        return (top,) + weighed(tiles, top * LOG2_SCALE)

    def with_chunk(state, block, chunk):
        top, row_total, gathered = state
        raw = scores_of(stacked_query(block), block, chunk - block)
        new_top = jnp.maximum(top, jnp.max(raw, axis=1, keepdims=True) + halo_bias)
        keep = jnp.exp2((top - new_top) * LOG2_SCALE)
        more_total, more = weighed([(chunk * TILE, raw)], new_top * LOG2_SCALE - halo_bias)
        return new_top, row_total * keep + more_total, gathered * keep + more

    def finish(block, state):
        _, row_total, gathered = state
        done = (gathered / row_total).astype(jnp.bfloat16)
        for part in range(QPK):
            o_rows[0, 0, block * TILE : (block + 1) * TILE, part * head : (part + 1) * head] = done[
                part * TILE : (part + 1) * TILE
            ]

    for load in loads:
        load.wait()

    states = [local_part(block) for block in range(q_blocks)]
    for block in range(chunks, q_blocks):
        finish(block, states[block])
    for chunk in reversed(range(chunks)):
        arrive(chunk)
        for block in range(chunk + 1):
            states[block] = with_chunk(states[block], block, chunk)
        finish(chunk, states[chunk])


def solution(mesh):
    seq_count = mesh.shape["seq"]
    mp_count = mesh.shape["mp"]

    def per_device(queries, key_rows, value_rows):
        rows = queries.shape[2]
        head = key_rows.shape[3]
        span = rows + WINDOW
        return pl.pallas_call(
            functools.partial(attention_kernel, seq_count, mp_count),
            out_shape=jax.ShapeDtypeStruct(queries.shape, jnp.bfloat16),
            in_specs=[pl.BlockSpec(memory_space=pltpu.HBM)] * 3,
            out_specs=pl.BlockSpec(memory_space=pltpu.VMEM),
            scratch_shapes=[
                pltpu.VMEM((rows, QPK * head), jnp.bfloat16),
                pltpu.VMEM((span, head), jnp.bfloat16),
                pltpu.VMEM((span, head), jnp.bfloat16),
                pltpu.SemaphoreType.DMA((3,)),
                pltpu.SemaphoreType.DMA((WINDOW // PIECE, 2)),
                pltpu.SemaphoreType.DMA((WINDOW // PIECE, 2)),
            ],
            compiler_params=pltpu.CompilerParams(
                collective_id=0, has_side_effects=True, vmem_limit_bytes=32 * 1024 * 1024
            ),
            cost_estimate=pl.CostEstimate(
                flops=4 * QPK * rows * (WINDOW + TILE) * head,
                bytes_accessed=6 * rows * QPK * head,
                transcendentals=QPK * rows * (WINDOW + TILE),
            ),
        )(*[pltpu.with_memory_space_constraint(x, pltpu.HBM) for x in (queries, key_rows, value_rows)])

    spec = P("seq", "mp", None, None)
    return jax.shard_map(per_device, mesh=mesh, in_specs=(spec, spec, spec), out_specs=spec, check_vma=False)
```

```python
import functools
import math

import jax
import jax.numpy as jnp
from jax import lax
from jax.experimental import pallas as pl
from jax.experimental.pallas import tpu as pltpu
from jax.sharding import PartitionSpec as P

KVH = 8
QPK = 2
WINDOW = 1024
TILE = 256
PIECE = 128
IN_FLIGHT = 5
LOG2_SCALE = 168.0 ** (-0.5) * math.log2(math.e)
LOWEST = -1e30


def attention_kernel(
    seq_count, mp_count, q_hbm, k_hbm, v_hbm, o_rows, q_rows, keys, values, in_sem, send_sem, recv_sem
):
    rows = q_hbm.shape[2]
    head = k_hbm.shape[3]
    blocks_here = mp_count // KVH
    total = seq_count * blocks_here
    chunks = WINDOW // TILE
    q_blocks = rows // TILE
    mp_index = lax.axis_index("mp")
    kv_head = mp_index % KVH
    group = lax.axis_index("seq") * blocks_here + mp_index // KVH
    opening = group == 0
    closing = group == total - 1

    def device_of(number):
        return (number // blocks_here, (number % blocks_here) * KVH + kv_head)

    following = device_of((group + 1) % total)
    previous = device_of((group + total - 1) % total)

    barrier = pltpu.get_barrier_semaphore()

    @pl.when(jnp.logical_not(opening))
    def _():
        pl.semaphore_signal(barrier, inc=1, device_id=previous, device_id_type=pl.DeviceIdType.MESH)

    loads = [
        pltpu.make_async_copy(k_hbm.at[0, 0], keys.at[pl.ds(WINDOW, rows)], in_sem.at[0]),
        pltpu.make_async_copy(q_hbm.at[0, 0], q_rows, in_sem.at[1]),
        pltpu.make_async_copy(v_hbm.at[0, 0], values.at[pl.ds(WINDOW, rows)], in_sem.at[2]),
    ]
    for load in loads:
        load.start()

    def halo_copies(piece):
        first = WINDOW - (piece + 1) * PIECE
        made = []
        for which, (source, target) in enumerate(((k_hbm, keys), (v_hbm, values))):
            made.append(
                pltpu.make_async_remote_copy(
                    src_ref=source.at[0, 0, pl.ds(rows - WINDOW + first, PIECE)],
                    dst_ref=target.at[pl.ds(first, PIECE)],
                    send_sem=send_sem.at[piece, which],
                    recv_sem=recv_sem.at[piece, which],
                    device_id=following,
                    device_id_type=pl.DeviceIdType.MESH,
                )
            )
        return made

    pieces = WINDOW // PIECE
    copies = [halo_copies(piece) for piece in range(pieces)]

    @pl.when(jnp.logical_not(closing))
    def _():
        pl.semaphore_wait(barrier, 1)
        for piece in range(min(IN_FLIGHT, pieces)):
            for copy in copies[piece]:
                copy.start()

    def sent(piece):
        @pl.when(jnp.logical_not(closing))
        def _():
            for copy in copies[piece]:
                copy.wait_send()
            if piece + IN_FLIGHT < pieces:
                for copy in copies[piece + IN_FLIGHT]:
                    copy.start()

    @pl.when(opening)
    def _():
        keys[0:WINDOW, :] = jnp.zeros((WINDOW, head), jnp.bfloat16)
        values[0:WINDOW, :] = jnp.zeros((WINDOW, head), jnp.bfloat16)

    halo_bias = jnp.where(opening, LOWEST, 0.0).astype(jnp.float32)

    def arrive(chunk):
        per_chunk = TILE // PIECE
        for piece in range((chunks - 1 - chunk) * per_chunk, (chunks - chunk) * per_chunk):

            @pl.when(jnp.logical_not(opening))
            def _():
                for copy in copies[piece]:
                    copy.wait_recv()

    stacked = QPK * TILE
    row_index = lax.broadcasted_iota(jnp.int32, (stacked, TILE), 0) % TILE
    column_index = lax.broadcasted_iota(jnp.int32, (stacked, TILE), 1)

    def scores_of(query, block, step):
        place = (block + step) * TILE
        raw = lax.dot_general(
            query, keys[place : place + TILE, :], (((1,), (1,)), ((), ())), preferred_element_type=jnp.float32
        )
        if step == 0:
            raw = jnp.where(column_index > row_index, raw, LOWEST)
        if step == chunks:
            raw = jnp.where(column_index <= row_index, raw, LOWEST)
        return raw

    def weighed(tiles, shift):
        lane_total = None
        gathered = None
        for place, raw in tiles:
            probable = jnp.exp2(raw * LOG2_SCALE - shift)
            lane_total = probable if lane_total is None else lane_total + probable
            term = jnp.dot(
                probable.astype(jnp.bfloat16), values[place : place + TILE, :], preferred_element_type=jnp.float32
            )
            gathered = term if gathered is None else gathered + term
        return jnp.sum(lane_total, axis=1, keepdims=True), gathered

    def stacked_query(block):
        both = q_rows[block * TILE : (block + 1) * TILE, :]
        return jnp.concatenate([both[:, part * head : (part + 1) * head] for part in range(QPK)], axis=0)

    def local_part(block):
        query = stacked_query(block)
        tiles = [
            ((block + step) * TILE, scores_of(query, block, step))
            for step in range(max(chunks - block, 0), chunks + 1)
        ]
        top = jnp.max(functools.reduce(jnp.maximum, [raw for _, raw in tiles]), axis=1, keepdims=True)
        return (top,) + weighed(tiles, top * LOG2_SCALE)

    def with_chunk(state, block, chunk):
        top, row_total, gathered = state
        raw = scores_of(stacked_query(block), block, chunk - block)
        new_top = jnp.maximum(top, jnp.max(raw, axis=1, keepdims=True) + halo_bias)
        keep = jnp.exp2((top - new_top) * LOG2_SCALE)
        more_total, more = weighed([(chunk * TILE, raw)], new_top * LOG2_SCALE - halo_bias)
        return new_top, row_total * keep + more_total, gathered * keep + more

    def finish(block, state):
        _, row_total, gathered = state
        done = (gathered / row_total).astype(jnp.bfloat16)
        for part in range(QPK):
            o_rows[0, 0, block * TILE : (block + 1) * TILE, part * head : (part + 1) * head] = done[
                part * TILE : (part + 1) * TILE
            ]

    for load in loads:
        load.wait()

    refills = iter(range(pieces))
    states = [None] * q_blocks
    for block in reversed(range(q_blocks)):
        states[block] = local_part(block)
        if block >= chunks:
            finish(block, states[block])
        if block == 2:
            sent(next(refills))
    sent(next(refills))
    for chunk in reversed(range(chunks)):
        arrive(chunk)
        for block in reversed(range(chunk + 1)):
            states[block] = with_chunk(states[block], block, chunk)
            if block == chunk:
                finish(chunk, states[chunk])
            if chunk == chunks - 1 and block == 2:
                sent(next(refills))
    for piece in refills:
        sent(piece)


def solution(mesh):
    seq_count = mesh.shape["seq"]
    mp_count = mesh.shape["mp"]

    def per_device(queries, key_rows, value_rows):
        rows = queries.shape[2]
        head = key_rows.shape[3]
        span = rows + WINDOW
        return pl.pallas_call(
            functools.partial(attention_kernel, seq_count, mp_count),
            out_shape=jax.ShapeDtypeStruct(queries.shape, jnp.bfloat16),
            in_specs=[pl.BlockSpec(memory_space=pltpu.HBM)] * 3,
            out_specs=pl.BlockSpec(memory_space=pltpu.VMEM),
            scratch_shapes=[
                pltpu.VMEM((rows, QPK * head), jnp.bfloat16),
                pltpu.VMEM((span, head), jnp.bfloat16),
                pltpu.VMEM((span, head), jnp.bfloat16),
                pltpu.SemaphoreType.DMA((3,)),
                pltpu.SemaphoreType.DMA((WINDOW // PIECE, 2)),
                pltpu.SemaphoreType.DMA((WINDOW // PIECE, 2)),
            ],
            compiler_params=pltpu.CompilerParams(
                collective_id=0, has_side_effects=True, vmem_limit_bytes=32 * 1024 * 1024
            ),
            cost_estimate=pl.CostEstimate(
                flops=4 * QPK * rows * (WINDOW + TILE) * head,
                bytes_accessed=6 * rows * QPK * head,
                transcendentals=QPK * rows * (WINDOW + TILE),
            ),
        )(*[pltpu.with_memory_space_constraint(x, pltpu.HBM) for x in (queries, key_rows, value_rows)])

    spec = P("seq", "mp", None, None)
    return jax.shard_map(per_device, mesh=mesh, in_specs=(spec, spec, spec), out_specs=spec, check_vma=False)
```

```python
import functools
import math

import jax
import jax.numpy as jnp
from jax import lax
from jax.experimental import pallas as pl
from jax.experimental.pallas import tpu as pltpu
from jax.sharding import PartitionSpec as P

KVH = 8
QPK = 2
WINDOW = 1024
TILE = 256
PIECE = 128
IN_FLIGHT = 5
LOG2_SCALE = 168.0 ** (-0.5) * math.log2(math.e)
LOWEST = -1e30


def tile_scores(query, key_tile, window_edge, causal_edge):
    raw = lax.dot_general(query, key_tile, (((1,), (1,)), ((), ())), preferred_element_type=jnp.float32)
    row_index = lax.broadcasted_iota(jnp.int32, raw.shape, 0) % TILE
    column_index = lax.broadcasted_iota(jnp.int32, raw.shape, 1)
    if window_edge:
        raw = jnp.where(column_index > row_index, raw, LOWEST)
    if causal_edge:
        raw = jnp.where(column_index <= row_index, raw, LOWEST)
    return raw


def weighed(tiles, shift):
    lane_total = None
    gathered = None
    for value_tile, raw in tiles:
        probable = jnp.exp2(raw * LOG2_SCALE - shift)
        lane_total = probable if lane_total is None else lane_total + probable
        term = jnp.dot(probable.astype(jnp.bfloat16), value_tile, preferred_element_type=jnp.float32)
        gathered = term if gathered is None else gathered + term
    return jnp.sum(lane_total, axis=1, keepdims=True), gathered


def merged(state, raw, value_tile, halo_bias):
    top, row_total, gathered = state
    new_top = jnp.maximum(top, jnp.max(raw, axis=1, keepdims=True) + halo_bias)
    keep = jnp.exp2((top - new_top) * LOG2_SCALE)
    more_total, more = weighed([(value_tile, raw)], new_top * LOG2_SCALE - halo_bias)
    return new_top, row_total * keep + more_total, gathered * keep + more


def divided(state):
    _, row_total, gathered = state
    return (gathered / row_total).astype(jnp.bfloat16)


def attention_kernel(
    seq_count, mp_count, q_hbm, k_hbm, v_hbm, o_rows, query_out, key_out, value_out, top_out, total_out, gathered_out,
    q_rows, keys, values, in_sem, send_sem, recv_sem
):
    rows = q_hbm.shape[2]
    head = k_hbm.shape[3]
    blocks_here = mp_count // KVH
    total = seq_count * blocks_here
    chunks = WINDOW // TILE
    q_blocks = rows // TILE
    mp_index = lax.axis_index("mp")
    kv_head = mp_index % KVH
    group = lax.axis_index("seq") * blocks_here + mp_index // KVH
    opening = group == 0
    closing = group == total - 1

    def device_of(number):
        return (number // blocks_here, (number % blocks_here) * KVH + kv_head)

    following = device_of((group + 1) % total)
    previous = device_of((group + total - 1) % total)

    barrier = pltpu.get_barrier_semaphore()

    @pl.when(jnp.logical_not(opening))
    def _():
        pl.semaphore_signal(barrier, inc=1, device_id=previous, device_id_type=pl.DeviceIdType.MESH)

    loads = [
        pltpu.make_async_copy(k_hbm.at[0, 0], keys.at[pl.ds(WINDOW, rows)], in_sem.at[0]),
        pltpu.make_async_copy(q_hbm.at[0, 0], q_rows, in_sem.at[1]),
        pltpu.make_async_copy(v_hbm.at[0, 0], values.at[pl.ds(WINDOW, rows)], in_sem.at[2]),
    ]
    for load in loads:
        load.start()

    def halo_copies(piece):
        first = WINDOW - (piece + 1) * PIECE
        made = []
        for which, (source, target) in enumerate(((k_hbm, keys), (v_hbm, values))):
            made.append(
                pltpu.make_async_remote_copy(
                    src_ref=source.at[0, 0, pl.ds(rows - WINDOW + first, PIECE)],
                    dst_ref=target.at[pl.ds(first, PIECE)],
                    send_sem=send_sem.at[piece, which],
                    recv_sem=recv_sem.at[piece, which],
                    device_id=following,
                    device_id_type=pl.DeviceIdType.MESH,
                )
            )
        return made

    pieces = WINDOW // PIECE
    copies = [halo_copies(piece) for piece in range(pieces)]

    @pl.when(jnp.logical_not(closing))
    def _():
        pl.semaphore_wait(barrier, 1)
        for piece in range(min(IN_FLIGHT, pieces)):
            for copy in copies[piece]:
                copy.start()

    def sent(piece):
        @pl.when(jnp.logical_not(closing))
        def _():
            for copy in copies[piece]:
                copy.wait_send()
            if piece + IN_FLIGHT < pieces:
                for copy in copies[piece + IN_FLIGHT]:
                    copy.start()

    @pl.when(opening)
    def _():
        keys[0:WINDOW, :] = jnp.zeros((WINDOW, head), jnp.bfloat16)
        values[0:WINDOW, :] = jnp.zeros((WINDOW, head), jnp.bfloat16)

    halo_bias = jnp.where(opening, LOWEST, 0.0).astype(jnp.float32)

    def arrive(chunk):
        per_chunk = TILE // PIECE
        for piece in range((chunks - 1 - chunk) * per_chunk, (chunks - chunk) * per_chunk):

            @pl.when(jnp.logical_not(opening))
            def _():
                for copy in copies[piece]:
                    copy.wait_recv()

    def scores_of(query, block, step):
        place = (block + step) * TILE
        return tile_scores(query, keys[place : place + TILE, :], step == 0, step == chunks)

    def stacked_query(block):
        both = q_rows[block * TILE : (block + 1) * TILE, :]
        return jnp.concatenate([both[:, part * head : (part + 1) * head] for part in range(QPK)], axis=0)

    def local_part(block):
        query = stacked_query(block)
        tiles = [
            (values[(block + step) * TILE : (block + step + 1) * TILE, :], scores_of(query, block, step))
            for step in range(max(chunks - block, 0), chunks + 1)
        ]
        top = jnp.max(functools.reduce(jnp.maximum, [raw for _, raw in tiles]), axis=1, keepdims=True)
        return (top,) + weighed(tiles, top * LOG2_SCALE)

    def with_chunk(state, block, chunk):
        value_tile = values[chunk * TILE : (chunk + 1) * TILE, :]
        return merged(state, scores_of(stacked_query(block), block, chunk - block), value_tile, halo_bias)

    def finish(block, state):
        done = divided(state)
        place = (block - 1) * TILE
        for part in range(QPK):
            o_rows[place : place + TILE, part * head : (part + 1) * head] = done[part * TILE : (part + 1) * TILE]

    for load in loads:
        load.wait()

    refills = iter(range(pieces))
    states = [None] * q_blocks
    for block in reversed(range(q_blocks)):
        states[block] = local_part(block)
        if block >= chunks:
            finish(block, states[block])
        if block == 2:
            sent(next(refills))
    sent(next(refills))
    for chunk in reversed(range(1, chunks)):
        arrive(chunk)
        for block in reversed(range(chunk + 1)):
            states[block] = with_chunk(states[block], block, chunk)
            if block == chunk:
                finish(chunk, states[chunk])
            if chunk == chunks - 1 and block == 2:
                sent(next(refills))
    query_out[...] = stacked_query(0)
    top_out[...], total_out[...], gathered_out[...] = states[0]
    arrive(0)
    key_out[...] = keys[0:TILE, :]
    value_out[...] = values[0:TILE, :]
    for piece in refills:
        sent(piece)


def closing_kernel(
    seq_count, mp_count, done_rows, query, key_tile, value_tile, top, row_total, gathered, o_hbm, first_rows, out_sem
):
    head = key_tile.shape[1]
    later = done_rows.shape[0] // TILE
    blocks_here = mp_count // KVH
    group = lax.axis_index("seq") * blocks_here + lax.axis_index("mp") // KVH
    halo_bias = jnp.where(group == 0, LOWEST, 0.0).astype(jnp.float32)
    copies = [
        pltpu.make_async_copy(
            done_rows.at[pl.ds(block * TILE, TILE)], o_hbm.at[0, 0, pl.ds((block + 1) * TILE, TILE)], out_sem.at[block]
        )
        for block in range(later)
    ]
    for copy in copies:
        copy.start()
    raw = tile_scores(query[...], key_tile[...], True, False)
    done = divided(merged((top[...], row_total[...], gathered[...]), raw, value_tile[...], halo_bias))
    for part in range(QPK):
        first_rows[:, part * head : (part + 1) * head] = done[part * TILE : (part + 1) * TILE]
    last = pltpu.make_async_copy(first_rows, o_hbm.at[0, 0, pl.ds(0, TILE)], out_sem.at[later])
    last.start()
    for copy in copies:
        copy.wait()
    last.wait()


def solution(mesh):
    seq_count = mesh.shape["seq"]
    mp_count = mesh.shape["mp"]

    def per_device(queries, key_rows, value_rows):
        rows = queries.shape[2]
        head = key_rows.shape[3]
        span = rows + WINDOW
        stacked = QPK * TILE
        whole = pl.BlockSpec(memory_space=pltpu.VMEM)
        held = pl.pallas_call(
            functools.partial(attention_kernel, seq_count, mp_count),
            out_shape=[
                jax.ShapeDtypeStruct((rows - TILE, QPK * head), jnp.bfloat16),
                jax.ShapeDtypeStruct((stacked, head), jnp.bfloat16),
                jax.ShapeDtypeStruct((TILE, head), jnp.bfloat16),
                jax.ShapeDtypeStruct((TILE, head), jnp.bfloat16),
                jax.ShapeDtypeStruct((stacked, 1), jnp.float32),
                jax.ShapeDtypeStruct((stacked, 1), jnp.float32),
                jax.ShapeDtypeStruct((stacked, head), jnp.float32),
            ],
            in_specs=[pl.BlockSpec(memory_space=pltpu.HBM)] * 3,
            out_specs=[whole] * 7,
            scratch_shapes=[
                pltpu.VMEM((rows, QPK * head), jnp.bfloat16),
                pltpu.VMEM((span, head), jnp.bfloat16),
                pltpu.VMEM((span, head), jnp.bfloat16),
                pltpu.SemaphoreType.DMA((3,)),
                pltpu.SemaphoreType.DMA((WINDOW // PIECE, 2)),
                pltpu.SemaphoreType.DMA((WINDOW // PIECE, 2)),
            ],
            compiler_params=pltpu.CompilerParams(
                collective_id=0, has_side_effects=True, vmem_limit_bytes=32 * 1024 * 1024
            ),
            cost_estimate=pl.CostEstimate(
                flops=4 * QPK * rows * (WINDOW + TILE) * head,
                bytes_accessed=6 * rows * QPK * head,
                transcendentals=QPK * rows * (WINDOW + TILE),
            ),
        )(*[pltpu.with_memory_space_constraint(x, pltpu.HBM) for x in (queries, key_rows, value_rows)])
        return pl.pallas_call(
            functools.partial(closing_kernel, seq_count, mp_count),
            out_shape=jax.ShapeDtypeStruct(queries.shape, jnp.bfloat16),
            in_specs=[whole] * 7,
            out_specs=pl.BlockSpec(memory_space=pltpu.HBM),
            scratch_shapes=[
                pltpu.VMEM((TILE, QPK * head), jnp.bfloat16),
                pltpu.SemaphoreType.DMA((rows // TILE,)),
            ],
            compiler_params=pltpu.CompilerParams(vmem_limit_bytes=16 * 1024 * 1024),
        )(*held)

    spec = P("seq", "mp", None, None)
    return jax.shard_map(per_device, mesh=mesh, in_specs=(spec, spec, spec), out_specs=spec, check_vma=False)
```

```python
import functools
import math

import jax
import jax.numpy as jnp
from jax import lax
from jax.experimental import pallas as pl
from jax.experimental.pallas import tpu as pltpu
from jax.sharding import PartitionSpec as P

KVH = 8
QPK = 2
WINDOW = 1024
TILE = 256
PIECE = 128
IN_FLIGHT = 5
LOG2_SCALE = 168.0 ** (-0.5) * math.log2(math.e)
LOWEST = -1e30


def attention_kernel(
    seq_count, mp_count, q_hbm, k_hbm, v_hbm, o_rows, q_rows, keys, values, in_sem, send_sem, recv_sem
):
    rows = q_hbm.shape[2]
    head = k_hbm.shape[3]
    blocks_here = mp_count // KVH
    total = seq_count * blocks_here
    chunks = WINDOW // TILE
    q_blocks = rows // TILE
    mp_index = lax.axis_index("mp")
    kv_head = mp_index % KVH
    group = lax.axis_index("seq") * blocks_here + mp_index // KVH
    opening = group == 0
    closing = group == total - 1

    def device_of(number):
        return (number // blocks_here, (number % blocks_here) * KVH + kv_head)

    following = device_of((group + 1) % total)
    previous = device_of((group + total - 1) % total)

    barrier = pltpu.get_barrier_semaphore()

    @pl.when(jnp.logical_not(opening))
    def _():
        pl.semaphore_signal(barrier, inc=1, device_id=previous, device_id_type=pl.DeviceIdType.MESH)

    loads = [
        pltpu.make_async_copy(k_hbm.at[0, 0], keys.at[pl.ds(WINDOW, rows)], in_sem.at[0]),
        pltpu.make_async_copy(q_hbm.at[0, 0], q_rows, in_sem.at[1]),
        pltpu.make_async_copy(v_hbm.at[0, 0], values.at[pl.ds(WINDOW, rows)], in_sem.at[2]),
    ]
    for load in loads:
        load.start()

    def halo_copies(piece):
        first = WINDOW - (piece + 1) * PIECE
        made = []
        for which, (source, target) in enumerate(((k_hbm, keys), (v_hbm, values))):
            made.append(
                pltpu.make_async_remote_copy(
                    src_ref=source.at[0, 0, pl.ds(rows - WINDOW + first, PIECE)],
                    dst_ref=target.at[pl.ds(first, PIECE)],
                    send_sem=send_sem.at[piece, which],
                    recv_sem=recv_sem.at[piece, which],
                    device_id=following,
                    device_id_type=pl.DeviceIdType.MESH,
                )
            )
        return made

    pieces = WINDOW // PIECE
    copies = [halo_copies(piece) for piece in range(pieces)]
    copies[-2:] = [list(group) for group in zip(*copies[-2:])]

    @pl.when(jnp.logical_not(closing))
    def _():
        pl.semaphore_wait(barrier, 1)
        for piece in range(min(IN_FLIGHT, pieces)):
            for copy in copies[piece]:
                copy.start()

    def sent(piece):
        @pl.when(jnp.logical_not(closing))
        def _():
            for copy in copies[piece]:
                copy.wait_send()
            if piece + IN_FLIGHT < pieces:
                for copy in copies[piece + IN_FLIGHT]:
                    copy.start()

    @pl.when(opening)
    def _():
        keys[0:WINDOW, :] = jnp.zeros((WINDOW, head), jnp.bfloat16)
        values[0:WINDOW, :] = jnp.zeros((WINDOW, head), jnp.bfloat16)

    halo_bias = jnp.where(opening, LOWEST, 0.0).astype(jnp.float32)

    def arrive(first, last):
        @pl.when(jnp.logical_not(opening))
        def _():
            for piece in range(first, last):
                for copy in copies[piece]:
                    copy.wait_recv()

    stacked = QPK * TILE
    row_index = lax.broadcasted_iota(jnp.int32, (stacked, TILE), 0) % TILE
    column_index = lax.broadcasted_iota(jnp.int32, (stacked, TILE), 1)

    def scores_of(query, block, step):
        place = (block + step) * TILE
        raw = lax.dot_general(
            query, keys[place : place + TILE, :], (((1,), (1,)), ((), ())), preferred_element_type=jnp.float32
        )
        if step == 0:
            raw = jnp.where(column_index > row_index, raw, LOWEST)
        if step == chunks:
            raw = jnp.where(column_index <= row_index, raw, LOWEST)
        return raw

    def weighed(tiles, shift):
        lane_total = None
        gathered = None
        for place, raw in tiles:
            probable = jnp.exp2(raw * LOG2_SCALE - shift)
            lane_total = probable if lane_total is None else lane_total + probable
            term = jnp.dot(
                probable.astype(jnp.bfloat16), values[place : place + TILE, :], preferred_element_type=jnp.float32
            )
            gathered = term if gathered is None else gathered + term
        return jnp.sum(lane_total, axis=1, keepdims=True), gathered

    def stacked_query(block):
        both = q_rows[block * TILE : (block + 1) * TILE, :]
        return jnp.concatenate([both[:, part * head : (part + 1) * head] for part in range(QPK)], axis=0)

    def local_part(block):
        query = stacked_query(block)
        tiles = [
            ((block + step) * TILE, scores_of(query, block, step))
            for step in range(max(chunks - block, 0), chunks + 1)
        ]
        top = jnp.max(functools.reduce(jnp.maximum, [raw for _, raw in tiles]), axis=1, keepdims=True)
        return (top,) + weighed(tiles, top * LOG2_SCALE)

    def with_chunk(state, block, chunk):
        top, row_total, gathered = state
        raw = scores_of(stacked_query(block), block, chunk - block)
        new_top = jnp.maximum(top, jnp.max(raw, axis=1, keepdims=True) + halo_bias)
        keep = jnp.exp2((top - new_top) * LOG2_SCALE)
        more_total, more = weighed([(chunk * TILE, raw)], new_top * LOG2_SCALE - halo_bias)
        return new_top, row_total * keep + more_total, gathered * keep + more

    def finish(block, state):
        _, row_total, gathered = state
        done = (gathered / row_total).astype(jnp.bfloat16)
        for part in range(QPK):
            o_rows[0, 0, block * TILE : (block + 1) * TILE, part * head : (part + 1) * head] = done[
                part * TILE : (part + 1) * TILE
            ]

    for load in loads:
        load.wait()

    refills = iter(range(pieces))
    states = [None] * q_blocks
    for block in reversed(range(q_blocks)):
        states[block] = local_part(block)
        if block >= chunks:
            finish(block, states[block])
        if block == 2:
            sent(next(refills))
    sent(next(refills))
    per_chunk = TILE // PIECE
    for chunk in reversed(range(1, chunks)):
        arrive((chunks - 1 - chunk) * per_chunk, (chunks - chunk) * per_chunk)
        for block in reversed(range(chunk + 1)):
            states[block] = with_chunk(states[block], block, chunk)
            if block == chunk:
                finish(chunk, states[chunk])
            if chunk == chunks - 1 and block == 2:
                sent(next(refills))
    top, row_total, gathered = states[0]
    query = stacked_query(0)
    arrive(pieces - 2, pieces - 1)
    raw = scores_of(query, 0, 0)
    new_top = jnp.maximum(top, jnp.max(raw, axis=1, keepdims=True) + halo_bias)
    keep = jnp.exp2((top - new_top) * LOG2_SCALE)
    probable = jnp.exp2(raw * LOG2_SCALE - (new_top * LOG2_SCALE - halo_bias))
    weights = probable.astype(jnp.bfloat16)
    row_total = row_total * keep + jnp.sum(probable, axis=1, keepdims=True)
    gathered = gathered * keep
    arrive(pieces - 1, pieces)
    gathered = gathered + jnp.dot(weights, values[0:TILE, :], preferred_element_type=jnp.float32)
    finish(0, (new_top, row_total, gathered))
    for piece in refills:
        sent(piece)


def solution(mesh):
    seq_count = mesh.shape["seq"]
    mp_count = mesh.shape["mp"]

    def per_device(queries, key_rows, value_rows):
        rows = queries.shape[2]
        head = key_rows.shape[3]
        span = rows + WINDOW
        return pl.pallas_call(
            functools.partial(attention_kernel, seq_count, mp_count),
            out_shape=jax.ShapeDtypeStruct(queries.shape, jnp.bfloat16),
            in_specs=[pl.BlockSpec(memory_space=pltpu.HBM)] * 3,
            out_specs=pl.BlockSpec(memory_space=pltpu.VMEM),
            scratch_shapes=[
                pltpu.VMEM((rows, QPK * head), jnp.bfloat16),
                pltpu.VMEM((span, head), jnp.bfloat16),
                pltpu.VMEM((span, head), jnp.bfloat16),
                pltpu.SemaphoreType.DMA((3,)),
                pltpu.SemaphoreType.DMA((WINDOW // PIECE, 2)),
                pltpu.SemaphoreType.DMA((WINDOW // PIECE, 2)),
            ],
            compiler_params=pltpu.CompilerParams(
                collective_id=0, has_side_effects=True, vmem_limit_bytes=32 * 1024 * 1024
            ),
            cost_estimate=pl.CostEstimate(
                flops=4 * QPK * rows * (WINDOW + TILE) * head,
                bytes_accessed=6 * rows * QPK * head,
                transcendentals=QPK * rows * (WINDOW + TILE),
            ),
        )(*[pltpu.with_memory_space_constraint(x, pltpu.HBM) for x in (queries, key_rows, value_rows)])

    spec = P("seq", "mp", None, None)
    return jax.shard_map(per_device, mesh=mesh, in_specs=(spec, spec, spec), out_specs=spec, check_vma=False)
```

```python
import functools
import math

import jax
import jax.numpy as jnp
from jax import lax
from jax.experimental import pallas as pl
from jax.experimental.pallas import tpu as pltpu
from jax.sharding import PartitionSpec as P

KVH = 8
QPK = 2
WINDOW = 1024
TILE = 256
PIECE = 128
IN_FLIGHT = (6, 4)
LOG2_SCALE = 168.0 ** (-0.5) * math.log2(math.e)
LOWEST = -1e30


def attention_kernel(
    seq_count, mp_count, q_hbm, k_hbm, v_hbm, o_rows, q_rows, keys, values, in_sem, send_sem, recv_sem
):
    rows = q_hbm.shape[2]
    head = k_hbm.shape[3]
    blocks_here = mp_count // KVH
    total = seq_count * blocks_here
    chunks = WINDOW // TILE
    q_blocks = rows // TILE
    mp_index = lax.axis_index("mp")
    kv_head = mp_index % KVH
    group = lax.axis_index("seq") * blocks_here + mp_index // KVH
    opening = group == 0
    closing = group == total - 1

    def device_of(number):
        return (number // blocks_here, (number % blocks_here) * KVH + kv_head)

    following = device_of((group + 1) % total)
    previous = device_of((group + total - 1) % total)

    barrier = pltpu.get_barrier_semaphore()

    @pl.when(jnp.logical_not(opening))
    def _():
        pl.semaphore_signal(barrier, inc=1, device_id=previous, device_id_type=pl.DeviceIdType.MESH)

    loads = [
        pltpu.make_async_copy(k_hbm.at[0, 0], keys.at[pl.ds(WINDOW, rows)], in_sem.at[0]),
        pltpu.make_async_copy(q_hbm.at[0, 0], q_rows, in_sem.at[1]),
        pltpu.make_async_copy(v_hbm.at[0, 0], values.at[pl.ds(WINDOW, rows)], in_sem.at[2]),
    ]
    for load in loads:
        load.start()

    def halo_copies(piece):
        first = WINDOW - (piece + 1) * PIECE
        made = []
        for which, (source, target) in enumerate(((k_hbm, keys), (v_hbm, values))):
            made.append(
                pltpu.make_async_remote_copy(
                    src_ref=source.at[0, 0, pl.ds(rows - WINDOW + first, PIECE)],
                    dst_ref=target.at[pl.ds(first, PIECE)],
                    send_sem=send_sem.at[piece, which],
                    recv_sem=recv_sem.at[piece, which],
                    device_id=following,
                    device_id_type=pl.DeviceIdType.MESH,
                )
            )
        return made

    pieces = WINDOW // PIECE
    copies = [halo_copies(piece) for piece in range(pieces)]
    copies[-2:] = [list(group) for group in zip(*copies[-2:])]

    @pl.when(jnp.logical_not(closing))
    def _():
        pl.semaphore_wait(barrier, 1)
        for piece in range(min(IN_FLIGHT)):
            for copy in copies[piece]:
                copy.start()

    @pl.when(jnp.logical_and(jnp.logical_not(closing), mp_index % 2 == 0))
    def _():
        for piece in range(min(IN_FLIGHT), IN_FLIGHT[0]):
            for copy in copies[piece]:
                copy.start()

    def sent(piece):
        @pl.when(jnp.logical_not(closing))
        def _():
            for copy in copies[piece]:
                copy.wait_send()

        for core, ahead in enumerate(IN_FLIGHT):
            if piece + ahead < pieces:

                @pl.when(jnp.logical_and(jnp.logical_not(closing), mp_index % 2 == core))
                def _():
                    for copy in copies[piece + ahead]:
                        copy.start()

    @pl.when(opening)
    def _():
        keys[0:WINDOW, :] = jnp.zeros((WINDOW, head), jnp.bfloat16)
        values[0:WINDOW, :] = jnp.zeros((WINDOW, head), jnp.bfloat16)

    halo_bias = jnp.where(opening, LOWEST, 0.0).astype(jnp.float32)

    def arrive(first, last):
        @pl.when(jnp.logical_not(opening))
        def _():
            for piece in range(first, last):
                for copy in copies[piece]:
                    copy.wait_recv()

    stacked = QPK * TILE
    row_index = lax.broadcasted_iota(jnp.int32, (stacked, TILE), 0) % TILE
    column_index = lax.broadcasted_iota(jnp.int32, (stacked, TILE), 1)

    def scores_of(query, block, step):
        place = (block + step) * TILE
        raw = lax.dot_general(
            query, keys[place : place + TILE, :], (((1,), (1,)), ((), ())), preferred_element_type=jnp.float32
        )
        if step == 0:
            raw = jnp.where(column_index > row_index, raw, LOWEST)
        if step == chunks:
            raw = jnp.where(column_index <= row_index, raw, LOWEST)
        return raw

    def weighed(tiles, shift):
        lane_total = None
        gathered = None
        for place, raw in tiles:
            probable = jnp.exp2(raw * LOG2_SCALE - shift)
            lane_total = probable if lane_total is None else lane_total + probable
            term = jnp.dot(
                probable.astype(jnp.bfloat16), values[place : place + TILE, :], preferred_element_type=jnp.float32
            )
            gathered = term if gathered is None else gathered + term
        return jnp.sum(lane_total, axis=1, keepdims=True), gathered

    def stacked_query(block):
        both = q_rows[block * TILE : (block + 1) * TILE, :]
        return jnp.concatenate([both[:, part * head : (part + 1) * head] for part in range(QPK)], axis=0)

    def local_part(block):
        query = stacked_query(block)
        tiles = [
            ((block + step) * TILE, scores_of(query, block, step))
            for step in range(max(chunks - block, 0), chunks + 1)
        ]
        top = jnp.max(functools.reduce(jnp.maximum, [raw for _, raw in tiles]), axis=1, keepdims=True)
        return (top,) + weighed(tiles, top * LOG2_SCALE)

    def with_chunk(state, block, chunk):
        top, row_total, gathered = state
        raw = scores_of(stacked_query(block), block, chunk - block)
        new_top = jnp.maximum(top, jnp.max(raw, axis=1, keepdims=True) + halo_bias)
        keep = jnp.exp2((top - new_top) * LOG2_SCALE)
        more_total, more = weighed([(chunk * TILE, raw)], new_top * LOG2_SCALE - halo_bias)
        return new_top, row_total * keep + more_total, gathered * keep + more

    def finish(block, state):
        _, row_total, gathered = state
        done = (gathered / row_total).astype(jnp.bfloat16)
        for part in range(QPK):
            o_rows[0, 0, block * TILE : (block + 1) * TILE, part * head : (part + 1) * head] = done[
                part * TILE : (part + 1) * TILE
            ]

    for load in loads:
        load.wait()

    refills = iter(range(pieces))
    states = [None] * q_blocks
    for block in reversed(range(q_blocks)):
        states[block] = local_part(block)
        if block >= chunks:
            finish(block, states[block])
        if block == 2:
            sent(next(refills))
    sent(next(refills))
    per_chunk = TILE // PIECE
    for chunk in reversed(range(1, chunks)):
        arrive((chunks - 1 - chunk) * per_chunk, (chunks - chunk) * per_chunk)
        for block in reversed(range(chunk + 1)):
            states[block] = with_chunk(states[block], block, chunk)
            if block == chunk:
                finish(chunk, states[chunk])
            if (chunk, block) in ((chunks - 1, 2), (chunks - 2, 1)):
                sent(next(refills))
    top, row_total, gathered = states[0]
    query = stacked_query(0)
    arrive(pieces - 2, pieces - 1)
    raw = scores_of(query, 0, 0)
    new_top = jnp.maximum(top, jnp.max(raw, axis=1, keepdims=True) + halo_bias)
    keep = jnp.exp2((top - new_top) * LOG2_SCALE)
    probable = jnp.exp2(raw * LOG2_SCALE - (new_top * LOG2_SCALE - halo_bias))
    weights = probable.astype(jnp.bfloat16)
    row_total = row_total * keep + jnp.sum(probable, axis=1, keepdims=True)
    gathered = gathered * keep
    arrive(pieces - 1, pieces)
    gathered = gathered + jnp.dot(weights, values[0:TILE, :], preferred_element_type=jnp.float32)
    finish(0, (new_top, row_total, gathered))
    for piece in refills:
        sent(piece)


def solution(mesh):
    seq_count = mesh.shape["seq"]
    mp_count = mesh.shape["mp"]

    def per_device(queries, key_rows, value_rows):
        rows = queries.shape[2]
        head = key_rows.shape[3]
        span = rows + WINDOW
        return pl.pallas_call(
            functools.partial(attention_kernel, seq_count, mp_count),
            out_shape=jax.ShapeDtypeStruct(queries.shape, jnp.bfloat16),
            in_specs=[pl.BlockSpec(memory_space=pltpu.HBM)] * 3,
            out_specs=pl.BlockSpec(memory_space=pltpu.VMEM),
            scratch_shapes=[
                pltpu.VMEM((rows, QPK * head), jnp.bfloat16),
                pltpu.VMEM((span, head), jnp.bfloat16),
                pltpu.VMEM((span, head), jnp.bfloat16),
                pltpu.SemaphoreType.DMA((3,)),
                pltpu.SemaphoreType.DMA((WINDOW // PIECE, 2)),
                pltpu.SemaphoreType.DMA((WINDOW // PIECE, 2)),
            ],
            compiler_params=pltpu.CompilerParams(
                collective_id=0, has_side_effects=True, vmem_limit_bytes=32 * 1024 * 1024
            ),
            cost_estimate=pl.CostEstimate(
                flops=4 * QPK * rows * (WINDOW + TILE) * head,
                bytes_accessed=6 * rows * QPK * head,
                transcendentals=QPK * rows * (WINDOW + TILE),
            ),
        )(*[pltpu.with_memory_space_constraint(x, pltpu.HBM) for x in (queries, key_rows, value_rows)])

    spec = P("seq", "mp", None, None)
    return jax.shard_map(per_device, mesh=mesh, in_specs=(spec, spec, spec), out_specs=spec, check_vma=False)
```
